32 devices in a mesh: inline: 4 (over y, core), xline: 8 (over z, x).
Axes of the slice: x: 2, y: 2, z: 4, core: 2. Of those that a mesh axis runs over, the one named last changes fastest.
Arguments:
- queries: bfloat16 [4, 8, 2, 64, 1024], P('inline', 'xline'), may hold values from -6 to 6
- keys: bfloat16 [4, 8, 2, 64, 1024], P('inline', 'xline'), may hold values from -6 to 6
- values: bfloat16 [4, 8, 2, 64, 1024], P('inline', 'xline'), may hold values from -6 to 6
- grad_out: bfloat16 [4, 8, 2, 64, 1024], P('inline', 'xline'), may hold values from -6 to 6
Outputs:
- grad_q: bfloat16 [4, 8, 2, 64, 1024], P('inline', 'xline')
- grad_k: bfloat16 [4, 8, 2, 64, 1024], P('inline', 'xline')
- grad_v: bfloat16 [4, 8, 2, 64, 1024], P('inline', 'xline')
The draws below stay inside these ranges and needn't reach their ends.
All inputs are finite; a program needn't handle non-finite values.
Results may differ from the reference program's by a relative error of at most 0.012.
Values may be sent and summed in bfloat16 or wider, within the bound.
A program may use at most 128 MiB of HBM per device.

```python
import math
import jax
import jax.numpy as jnp
from jax import lax

H = 16
HD = 64
TILE = 64
TZ = 2
TX = 4
TY = 8


def base_draw(key, salt):
    sub_key = jax.random.fold_in(key, salt)
    shape = (TX, TY, TZ, TILE, H * HD)
    return jax.random.truncated_normal(sub_key, -6.0, 6.0, shape, jnp.float32)


def draw_queries(key, part):
    entries = base_draw(key, 1)
    return entries.astype(jnp.bfloat16)


def draw_keys(key, part):
    entries = base_draw(key, 2)
    return entries.astype(jnp.bfloat16)


def steps_of(own_key, dims, shards, low, largest):
    factor_of, own = 1.0, jax.random.fold_in(own_key, 6)
    for axis_at, shards_of in shards:
        steps = jnp.exp(jax.random.uniform(jax.random.fold_in(own, axis_at), (shards_of,), jnp.float32, low / len(shards), largest / len(shards)))
        factor_of = factor_of * jnp.repeat(steps, dims[axis_at] // shards_of).reshape([-1 if axis == axis_at else 1 for axis in range(len(dims))])
    return factor_of


def scatter_about(stream_key, extent, scale, bound, split=(), held_as=jnp.bfloat16):
    factor_of = steps_of(stream_key, extent, split, -0.22, 0.18) if split else 1.0
    values = jax.random.normal(stream_key, extent, jnp.float32) * scale * factor_of
    return jnp.minimum(jnp.maximum(values, -bound), bound).astype(held_as)


def setup_inputs(seed: int = 0) -> dict:
    key_list = jax.random.split(jax.random.key(seed), 5)
    queries = draw_queries(jax.random.fold_in(key_list[4], 71), 0)
    keys = draw_keys(jax.random.fold_in(key_list[4], 71), 0)
    values = scatter_about(key_list[2], (TX, TY, TZ, TILE, H * HD), 1.0, 6.0, ((0, 4), (1, 8)))
    grad_out = scatter_about(key_list[3], (TX, TY, TZ, TILE, H * HD), 1.0, 6.0, ((0, 4), (1, 8)))
    return dict(queries=queries, keys=keys, values=values, grad_out=grad_out)


NEG_FILL = -1e+30

def window_offsets():
    return [(shift_x, shift_y, shift_z) for shift_x in range(3) for shift_y in range(3) for shift_z in range(3)]

def tile_grads(query_rows, grad_rows, key_win, value_win, inside):
    scaling = 1.0 / math.sqrt(query_rows.shape[-1])
    query_wide = query_rows.astype(jnp.float32)
    grad_wide = grad_rows.astype(jnp.float32)
    key_wide = key_win.astype(jnp.float32)
    value_wide = value_win.astype(jnp.float32)
    scores = jnp.einsum('nqd,nkd->nqk', query_wide, key_wide) * scaling
    scores = jnp.where(inside, scores, NEG_FILL)
    row_max = lax.optimization_barrier(jnp.max(scores, axis=-1))
    row_total = lax.optimization_barrier(jnp.sum(jnp.exp(scores - row_max[..., None]), axis=-1))
    log_norm = row_max + jnp.log(row_total)
    weights = jnp.exp(scores - log_norm[..., None])
    weights_low = weights.astype(jnp.bfloat16).astype(jnp.float32)
    attended = jnp.einsum('nqk,nkd->nqd', weights_low, value_wide)
    row_dot = lax.optimization_barrier(jnp.sum(grad_wide * attended, axis=-1))
    dprobs = jnp.einsum('nqd,nkd->nqk', grad_wide, value_wide)
    dscores = (weights * (dprobs - row_dot[..., None])).astype(jnp.bfloat16).astype(jnp.float32)
    grad_query = jnp.einsum('nqk,nkd->nqd', dscores, key_wide) * scaling
    grad_key = jnp.einsum('nqk,nqd->nkd', dscores, query_wide) * scaling
    grad_value = jnp.einsum('nqk,nqd->nkd', weights_low, grad_wide)
    return (grad_query, grad_key, grad_value)

def reference(queries, keys, values, grad_out):
    offsets = window_offsets()
    offset_table = jnp.array(offsets, jnp.int32)
    count_slots = len(offsets)

    def split_heads(array):
        return array.reshape(TX, TY, TZ, TILE, H, HD).transpose(4, 0, 1, 2, 3, 5)
    pos_y = jnp.arange(TY, dtype=jnp.int32)[:, None, None] + offset_table[:, 1] - 1
    pos_z = jnp.arange(TZ, dtype=jnp.int32)[None, :, None] + offset_table[:, 2] - 1

    def one_head(operands):
        query_h, key_h, value_h, grad_h = operands
        padded = jnp.pad(jnp.stack([key_h, value_h]), ((0, 0), (1, 1), (1, 1), (1, 1), (0, 0), (0, 0)))
        totals = jnp.zeros((2, TX + 2, TY + 2, TZ + 2, TILE, HD), jnp.float32)

        def sweep_step(totals, plane_x):
            key_slab = lax.dynamic_slice_in_dim(padded, plane_x, 3, 1)
            windows = jnp.stack([key_slab[:, shift_x, shift_y:shift_y + TY, shift_z:shift_z + TZ] for shift_x, shift_y, shift_z in offsets], axis=3)
            windows = windows.reshape(2, TY * TZ, count_slots * TILE, HD)
            pos_x = plane_x + offset_table[:, 0] - 1
            inside = (pos_x >= 0) & (pos_x < TX) & (pos_y >= 0) & (pos_y < TY) & (pos_z >= 0) & (pos_z < TZ)
            inside = jnp.broadcast_to(inside[..., None], (TY, TZ, count_slots, TILE)).reshape(TY * TZ, 1, count_slots * TILE)
            query_rows = lax.dynamic_index_in_dim(query_h, plane_x, 0, keepdims=False).reshape(TY * TZ, TILE, HD)
            grad_rows = lax.dynamic_index_in_dim(grad_h, plane_x, 0, keepdims=False).reshape(TY * TZ, TILE, HD)
            grad_query, grad_key, grad_value = tile_grads(query_rows, grad_rows, windows[0], windows[1], inside)
            deposits = jnp.stack([grad_key, grad_value]).reshape(2, TY, TZ, count_slots, TILE, HD)
            deposit = jnp.zeros((2, 3, TY + 2, TZ + 2, TILE, HD), jnp.float32)
            for slot_index, (shift_x, shift_y, shift_z) in enumerate(offsets):
                deposit = deposit.at[:, shift_x, shift_y:shift_y + TY, shift_z:shift_z + TZ].add(deposits[:, :, :, slot_index])
            current = lax.dynamic_slice_in_dim(totals, plane_x, 3, 1) + deposit
            totals = lax.dynamic_update_slice_in_dim(totals, current, plane_x, 1)
            return (totals, grad_query.astype(jnp.bfloat16).reshape(TY, TZ, TILE, HD))
        totals, grad_query = lax.scan(sweep_step, totals, jnp.arange(TX, dtype=jnp.int32))
        interior = totals[:, 1:TX + 1, 1:TY + 1, 1:TZ + 1].astype(jnp.bfloat16)
        return (grad_query, interior[0], interior[1])
    results = lax.map(one_head, (split_heads(queries), split_heads(keys), split_heads(values), split_heads(grad_out)))

    def to_tokens(array):
        return array.transpose(1, 2, 3, 4, 0, 5).reshape(TX, TY, TZ, TILE, H * HD)
    return (to_tokens(results[0]), to_tokens(results[1]), to_tokens(results[2]))
```

```python
import functools
import math

import jax
import jax.numpy as jnp
from jax import lax
from jax.experimental import pallas as pl
from jax.experimental.pallas import tpu as pltpu
from jax.sharding import PartitionSpec as P

HD = 64
LANES = 128
NEG_FILL = -1e30
MESH = pl.DeviceIdType.MESH


def attention_kernel(
    cols, rows, groups, tokens, width, heads,
    q_ref, k_ref, v_ref, g_ref, dq_ref, dk_ref, dv_ref,
    qg, kv, acc, dq_out, kv_out, term_out, term_in,
    in_send, in_recv, halo_send, halo_recv, term_send, term_recv, out_send, out_recv,
):
    members = rows * cols
    scale = 1.0 / math.sqrt(HD)
    my_col = lax.axis_index("inline")
    my_y = lax.axis_index("xline")
    group = my_y // rows
    base_y = group * rows
    me_row = my_y - base_y
    me = me_row * cols + my_col
    has_above = group > 0
    has_below = group < groups - 1
    above = (my_col, jnp.maximum(my_y - rows, 0))
    below = (my_col, jnp.minimum(my_y + rows, groups * rows - 1))
    sides = ((has_above, above), (has_below, below))

    def chunk(ref, member):
        if width % LANES == 0:
            return ref.at[:, pl.ds(pl.multiple_of(member * width, LANES), width)]
        return ref.at[member]

    def remote(src, dst, send, recv, device):
        return pltpu.make_async_remote_copy(
            src_ref=src, dst_ref=dst, send_sem=send, recv_sem=recv,
            device_id=device, device_id_type=MESH,
        )

    def arrived(dst, sem):
        pltpu.make_async_copy(dst, dst, sem).wait()

    def partner(step):
        member = lax.rem(me + step, members)
        row = member // cols
        return member, (member - row * cols, base_y + row)

    barrier = pltpu.get_barrier_semaphore()
    for step in range(1, members):
        pl.semaphore_signal(barrier, inc=1, device_id=partner(step)[1], device_id_type=MESH)
    for present, device in sides:
        @pl.when(present)
        def _():
            pl.semaphore_signal(barrier, inc=1, device_id=device, device_id_type=MESH)
    pl.semaphore_wait(
        barrier, members - 1 + has_above.astype(jnp.int32) + has_below.astype(jnp.int32)
    )

    inputs = ((k_ref, 0), (v_ref, 1), (q_ref, 2), (g_ref, 3))

    def slot(array, row, col):
        return kv.at[array, row + 1, col] if array < 2 else qg.at[array - 2, row, col]

    def in_copy(ref, array, step):
        member, device = partner(step)
        return remote(
            chunk(ref, member), slot(array, me_row, my_col),
            in_send.at[array, step], in_recv.at[array, me], device,
        )

    for ref, array in inputs:
        for step in range(1, members):
            in_copy(ref, array, step).start()
        pltpu.make_async_copy(
            chunk(ref, me), slot(array, me_row, my_col), in_recv.at[array, me]
        ).start()

    acc[...] = jnp.zeros_like(acc)
    for side, (present, _) in enumerate(sides):
        @pl.when(jnp.logical_not(present))
        def _():
            for array in range(2):
                kv[array, side * (rows + 1)] = jnp.zeros_like(kv[array, 0])
                term_in[array, side] = jnp.zeros_like(term_in[array, side])

    def halo_copy(array, side, col):
        return remote(
            kv.at[array, 1 if side == 0 else rows, col],
            kv.at[array, rows + 1 if side == 0 else 0, col],
            halo_send.at[array, side, col], halo_recv.at[array, 1 - side, col],
            sides[side][1],
        )

    for array in range(2):
        for col in range(cols):
            for row in range(rows):
                arrived(slot(array, row, col), in_recv.at[array, row * cols + col])
            for side in range(2):
                @pl.when(sides[side][0])
                def _():
                    halo_copy(array, side, col).start()

    def await_halo(col):
        for array in range(2):
            for side in range(2):
                @pl.when(sides[side][0])
                def _():
                    arrived(kv.at[array, side * (rows + 1), col], halo_recv.at[array, side, col])

    lane = lax.broadcasted_iota(jnp.int32, (tokens, width), 1)

    def by_head(block, factor):
        wide = block.astype(jnp.float32) * factor
        if heads == 1:
            return wide.astype(jnp.bfloat16)
        return jnp.concatenate(
            [
                jnp.where((lane >= h * HD) & (lane < (h + 1) * HD), wide, 0.0).astype(jnp.bfloat16)
                for h in range(heads)
            ],
            axis=0,
        )

    def dot(a, b, contract):
        return lax.dot_general(
            a, b, ((contract[:1], contract[1:]), ((), ())), preferred_element_type=jnp.float32
        )

    def tile(row, col):
        first, last = max(col - 1, 0), min(col + 1, cols - 1)
        count = last - first + 1
        query = by_head(qg[0, row, col], scale)
        grad = by_head(qg[1, row, col], 1.0)
        key_rows = range(row, row + 3)

        def present(key_row):
            if key_row == 0:
                return has_above
            return has_below if key_row == rows + 1 else None

        def window(array, key_row):
            return kv[array, key_row, first : last + 1].reshape(count * tokens, width)

        scores = [dot(window(0, key_row), query, (1, 1)) for key_row in key_rows]
        peak = None
        for key_row, part in zip(key_rows, scores):
            part_peak = jnp.max(part, axis=0, keepdims=True)
            if present(key_row) is not None:
                part_peak = jnp.where(present(key_row), part_peak, NEG_FILL)
            peak = part_peak if peak is None else jnp.maximum(peak, part_peak)
        weights = []
        total = jnp.zeros_like(peak)
        for key_row, part in zip(key_rows, scores):
            shift = peak
            if present(key_row) is not None:
                shift = jnp.where(present(key_row), peak, -NEG_FILL)
            weights.append(jnp.exp(part - shift))
            total = total + jnp.sum(weights[-1], axis=0, keepdims=True)
        inverse = 1.0 / total
        row_dot = jnp.zeros_like(peak)
        dprobs = []
        for index, key_row in enumerate(key_rows):
            weights[index] = weights[index] * inverse
            dprobs.append(dot(window(1, key_row), grad, (1, 1)))
            row_dot = row_dot + jnp.sum(weights[index] * dprobs[index], axis=0, keepdims=True)
        turned = None
        for index, key_row in enumerate(key_rows):
            dscores = (weights[index] * (dprobs[index] - row_dot)).astype(jnp.bfloat16)
            low = weights[index].astype(jnp.bfloat16)
            block = (slice(None), slice(None))
            grad_key = dot(dscores, query, (1, 0)).reshape(count, tokens, width)
            acc[(0, key_row, slice(first, last + 1)) + block] += grad_key
            grad_value = dot(low, grad, (1, 0)).reshape(count, tokens, width)
            acc[(1, key_row, slice(first, last + 1)) + block] += grad_value
            term = dot(window(0, key_row), dscores, (0, 0))
            turned = term if turned is None else turned + term
        picked = jnp.concatenate(
            [turned[h * HD : (h + 1) * HD, h * tokens : (h + 1) * tokens] for h in range(heads)],
            axis=0,
        )
        dq_out[row, col] = (picked.T * scale).astype(jnp.bfloat16)

    outs = (dq_ref, dk_ref, dv_ref)

    def out_src(array, row, col):
        return dq_out.at[row, col] if array == 0 else kv_out.at[array - 1, row, col]

    def out_copy(array, row, col):
        return remote(
            out_src(array, row, col), chunk(outs[array], me),
            out_send.at[array, row, col], out_recv.at[array, me], (col, base_y + row),
        )

    def deliver(array, row, col):
        own = me == row * cols + col

        @pl.when(own)
        def _():
            pltpu.make_async_copy(
                out_src(array, row, col), chunk(outs[array], me), out_recv.at[array, me]
            ).start()

        @pl.when(jnp.logical_not(own))
        def _():
            out_copy(array, row, col).start()

    def term_copy(array, side, col):
        return remote(
            term_out.at[array, side, col], term_in.at[array, 1 - side, col],
            term_send.at[array, side, col], term_recv.at[array, 1 - side, col],
            sides[side][1],
        )

    def send_terms(col):
        for array in range(2):
            for side in range(2):
                @pl.when(sides[side][0])
                def _():
                    term_out[array, side, col] = acc[array, side * (rows + 1), col].astype(
                        jnp.bfloat16
                    )
                    term_copy(array, side, col).start()

    def finish(col):
        for array in range(2):
            for side in range(2):
                @pl.when(sides[side][0])
                def _():
                    arrived(term_in.at[array, side, col], term_recv.at[array, side, col])
            for row in range(rows):
                total = acc[array, row + 1, col]
                if row == 0:
                    total = total + term_in[array, 0, col].astype(jnp.float32)
                if row == rows - 1:
                    total = total + term_in[array, 1, col].astype(jnp.float32)
                kv_out[array, row, col] = total.astype(jnp.bfloat16)
                deliver(array + 1, row, col)

    await_halo(0)
    for col in range(cols):
        if col + 1 < cols:
            await_halo(col + 1)
        for row in range(rows):
            for array in (2, 3):
                arrived(slot(array, row, col), in_recv.at[array, row * cols + col])
            tile(row, col)
            deliver(0, row, col)
        if col >= 1:
            send_terms(col - 1)
        if col >= 2:
            finish(col - 2)
    send_terms(cols - 1)
    for col in range(max(cols - 2, 0), cols):
        finish(col)

    for ref, array in inputs:
        for step in range(1, members):
            in_copy(ref, array, step).wait_send()
    for array in range(2):
        for side in range(2):
            for col in range(cols):
                @pl.when(sides[side][0])
                def _():
                    halo_copy(array, side, col).wait_send()
                    term_copy(array, side, col).wait_send()
    for array in range(3):
        for row in range(rows):
            for col in range(cols):
                @pl.when(me != row * cols + col)
                def _():
                    out_copy(array, row, col).wait_send()
        for member in range(members):
            arrived(chunk(outs[array], member), out_recv.at[array, member])


def shards(rows, cols, groups, queries, keys, values, grad_out):
    shape = queries.shape
    tokens, full = shape[2] * shape[3], shape[4]
    members = rows * cols
    width = full // members
    heads = width // HD

    def pack(array):
        array = array.reshape(tokens, full)
        if width % LANES == 0:
            return array
        return array.reshape(tokens, members, width).transpose(1, 0, 2)

    def unpack(array):
        if width % LANES:
            array = array.transpose(1, 0, 2)
        return array.reshape(shape)

    packed = (tokens, full) if width % LANES == 0 else (members, tokens, width)
    low, wide = jnp.bfloat16, jnp.float32
    dma = pltpu.SemaphoreType.DMA
    outputs = pl.pallas_call(
        functools.partial(attention_kernel, cols, rows, groups, tokens, width, heads),
        out_shape=[jax.ShapeDtypeStruct(packed, low)] * 3,
        in_specs=[pl.BlockSpec(memory_space=pl.ANY)] * 4,
        out_specs=[pl.BlockSpec(memory_space=pl.ANY)] * 3,
        scratch_shapes=[
            pltpu.VMEM((2, rows, cols, tokens, width), low),
            pltpu.VMEM((2, rows + 2, cols, tokens, width), low),
            pltpu.VMEM((2, rows + 2, cols, tokens, width), wide),
            pltpu.VMEM((rows, cols, tokens, width), low),
            pltpu.VMEM((2, rows, cols, tokens, width), low),
            pltpu.VMEM((2, 2, cols, tokens, width), low),
            pltpu.VMEM((2, 2, cols, tokens, width), low),
            dma((4, members)),
            dma((4, members)),
            dma((2, 2, cols)),
            dma((2, 2, cols)),
            dma((2, 2, cols)),
            dma((2, 2, cols)),
            dma((3, rows, cols)),
            dma((3, members)),
        ],
        compiler_params=pltpu.CompilerParams(
            collective_id=0, has_side_effects=True, vmem_limit_bytes=48 * 1024 * 1024
        ),
    )(pack(queries), pack(keys), pack(values), pack(grad_out))
    return tuple(unpack(array) for array in outputs)


def solution(mesh):
    cols, lines = mesh.shape["inline"], mesh.shape["xline"]
    spec = P("inline", "xline", None, None, None)

    def body(queries, keys, values, grad_out):
        heads = queries.shape[4] // HD
        rows = 2 if heads % (2 * cols) == 0 and lines % 2 == 0 else 1
        return shards(rows, cols, lines // rows, queries, keys, values, grad_out)

    return jax.shard_map(
        body, mesh=mesh, in_specs=(spec,) * 4, out_specs=(spec,) * 3, check_vma=False
    )
```

```python
import functools
import math

import jax
import jax.numpy as jnp
from jax import lax
from jax.experimental import pallas as pl
from jax.experimental.pallas import tpu as pltpu
from jax.sharding import PartitionSpec as P

HD = 64
LANES = 128
NEG_FILL = -1e30
MESH = pl.DeviceIdType.MESH


def attention_kernel(
    cols, rows, groups, tokens, width, heads,
    q_ref, k_ref, v_ref, g_ref, dq_ref, dk_ref, dv_ref,
    qg, kv, acc, weights, query_heads, grad_heads, dq_out, kv_out, term_out, term_in,
    in_send, in_recv, halo_send, halo_recv, term_send, term_recv, out_send, out_recv,
):
    members = rows * cols
    scale = 1.0 / math.sqrt(HD)
    my_col = lax.axis_index("inline")
    my_y = lax.axis_index("xline")
    group = my_y // rows
    base_y = group * rows
    me_row = my_y - base_y
    me = me_row * cols + my_col
    has_above = group > 0
    has_below = group < groups - 1
    above = (my_col, jnp.maximum(my_y - rows, 0))
    below = (my_col, jnp.minimum(my_y + rows, groups * rows - 1))
    sides = ((has_above, above), (has_below, below))

    def chunk(ref, member):
        if width % LANES == 0:
            return ref.at[:, pl.ds(pl.multiple_of(member * width, LANES), width)]
        return ref.at[member]

    def remote(src, dst, send, recv, device):
        return pltpu.make_async_remote_copy(
            src_ref=src, dst_ref=dst, send_sem=send, recv_sem=recv,
            device_id=device, device_id_type=MESH,
        )

    def arrived(dst, sem):
        pltpu.make_async_copy(dst, dst, sem).wait()

    def partner(step):
        member = lax.rem(me + step, members)
        row = member // cols
        return member, (member - row * cols, base_y + row)

    barrier = pltpu.get_barrier_semaphore()
    for step in range(1, members):
        pl.semaphore_signal(barrier, inc=1, device_id=partner(step)[1], device_id_type=MESH)
    for present, device in sides:
        @pl.when(present)
        def _():
            pl.semaphore_signal(barrier, inc=1, device_id=device, device_id_type=MESH)
    pl.semaphore_wait(
        barrier, members - 1 + has_above.astype(jnp.int32) + has_below.astype(jnp.int32)
    )

    inputs = ((k_ref, 0), (q_ref, 2), (v_ref, 1), (g_ref, 3))

    def slot(array, row, col):
        return kv.at[array, row + 1, col] if array < 2 else qg.at[array - 2, row, col]

    def in_copy(ref, array, step):
        member, device = partner(step)
        return remote(
            chunk(ref, member), slot(array, me_row, my_col),
            in_send.at[array, step], in_recv.at[array, me], device,
        )

    def spread(index):
        ref, array = inputs[index]
        for step in range(1, members):
            in_copy(ref, array, step).start()
        pltpu.make_async_copy(
            chunk(ref, me), slot(array, me_row, my_col), in_recv.at[array, me]
        ).start()

    spread(0)
    spread(1)

    acc[...] = jnp.zeros_like(acc)
    for side, (present, _) in enumerate(sides):
        @pl.when(jnp.logical_not(present))
        def _():
            for array in range(2):
                kv[array, side * (rows + 1)] = jnp.zeros_like(kv[array, 0])
                term_in[array, side] = jnp.zeros_like(term_in[array, side])

    def halo_copy(array, side, col):
        return remote(
            kv.at[array, 1 if side == 0 else rows, col],
            kv.at[array, rows + 1 if side == 0 else 0, col],
            halo_send.at[array, side, col], halo_recv.at[array, 1 - side, col],
            sides[side][1],
        )

    def forward(array):
        for col in range(cols):
            for row in range(rows):
                arrived(slot(array, row, col), in_recv.at[array, row * cols + col])
            for side in range(2):
                @pl.when(sides[side][0])
                def _():
                    halo_copy(array, side, col).start()

    def await_halo(array, col):
        if col >= cols:
            return
        for side in range(2):
            @pl.when(sides[side][0])
            def _():
                arrived(kv.at[array, side * (rows + 1), col], halo_recv.at[array, side, col])

    lane = lax.broadcasted_iota(jnp.int32, (tokens, width), 1)

    def by_head(block, factor):
        wide = block.astype(jnp.float32) * factor
        if heads == 1:
            return wide.astype(jnp.bfloat16)
        return jnp.concatenate(
            [
                jnp.where((lane >= h * HD) & (lane < (h + 1) * HD), wide, 0.0).astype(jnp.bfloat16)
                for h in range(heads)
            ],
            axis=0,
        )

    def dot(a, b, contract):
        return lax.dot_general(
            a, b, ((contract[:1], contract[1:]), ((), ())), preferred_element_type=jnp.float32
        )

    def span(col):
        first, last = max(col - 1, 0), min(col + 1, cols - 1)
        return first, last - first + 1

    def window(array, key_row, col):
        first, count = span(col)
        return kv[array, key_row, first : first + count].reshape(count * tokens, width)

    def present(key_row):
        if key_row == 0:
            return has_above
        return has_below if key_row == rows + 1 else None

    def softmax(row, col):
        _, count = span(col)
        query = by_head(qg[0, row, col], scale)
        query_heads[row, col] = query
        key_rows = range(row, row + 3)
        scores = [dot(window(0, key_row, col), query, (1, 1)) for key_row in key_rows]
        peak = None
        for key_row, part in zip(key_rows, scores):
            part_peak = jnp.max(part, axis=0, keepdims=True)
            if present(key_row) is not None:
                part_peak = jnp.where(present(key_row), part_peak, NEG_FILL)
            peak = part_peak if peak is None else jnp.maximum(peak, part_peak)
        terms = []
        total = jnp.zeros_like(peak)
        for key_row, part in zip(key_rows, scores):
            shift = peak
            if present(key_row) is not None:
                shift = jnp.where(present(key_row), peak, -NEG_FILL)
            terms.append(jnp.exp(part - shift))
            total = total + jnp.sum(terms[-1], axis=0, keepdims=True)
        inverse = 1.0 / total
        for index in range(3):
            weights[row, col, index, : count * tokens] = terms[index] * inverse

    def value_gradient(row, col):
        first, count = span(col)
        grad = by_head(qg[1, row, col], 1.0)
        grad_heads[row, col] = grad
        for index in range(3):
            low = weights[row, col, index, : count * tokens].astype(jnp.bfloat16)
            term = dot(low, grad, (1, 0)).reshape(count, tokens, width)
            acc[1, row + index, first : first + count] += term

    def gradients(row, col):
        first, count = span(col)
        query = query_heads[row, col]
        grad = grad_heads[row, col]
        row_dot = None
        dprobs = []
        probs = [weights[row, col, index, : count * tokens] for index in range(3)]
        for index in range(3):
            dprobs.append(dot(window(1, row + index, col), grad, (1, 1)))
            part_dot = jnp.sum(probs[index] * dprobs[index], axis=0, keepdims=True)
            row_dot = part_dot if row_dot is None else row_dot + part_dot
        turned = None
        for index in range(3):
            key_row = row + index
            dscores = (probs[index] * (dprobs[index] - row_dot)).astype(jnp.bfloat16)
            grad_key = dot(dscores, query, (1, 0)).reshape(count, tokens, width)
            acc[0, key_row, first : first + count] += grad_key
            term = dot(window(0, key_row, col), dscores, (0, 0))
            turned = term if turned is None else turned + term
        picked = jnp.concatenate(
            [turned[h * HD : (h + 1) * HD, h * tokens : (h + 1) * tokens] for h in range(heads)],
            axis=0,
        )
        dq_out[row, col] = (picked.T * scale).astype(jnp.bfloat16)

    outs = (dq_ref, dk_ref, dv_ref)

    def out_src(array, row, col):
        return dq_out.at[row, col] if array == 0 else kv_out.at[array - 1, row, col]

    def out_copy(array, row, col):
        return remote(
            out_src(array, row, col), chunk(outs[array], me),
            out_send.at[array, row, col], out_recv.at[array, me], (col, base_y + row),
        )

    def deliver(array, row, col):
        own = me == row * cols + col

        @pl.when(own)
        def _():
            pltpu.make_async_copy(
                out_src(array, row, col), chunk(outs[array], me), out_recv.at[array, me]
            ).start()

        @pl.when(jnp.logical_not(own))
        def _():
            out_copy(array, row, col).start()

    def term_copy(array, side, col):
        return remote(
            term_out.at[array, side, col], term_in.at[array, 1 - side, col],
            term_send.at[array, side, col], term_recv.at[array, 1 - side, col],
            sides[side][1],
        )

    def send_terms(array, col):
        for side in range(2):
            @pl.when(sides[side][0])
            def _():
                term_out[array, side, col] = acc[array, side * (rows + 1), col].astype(
                    jnp.bfloat16
                )
                term_copy(array, side, col).start()

    def finish(array, col):
        for side in range(2):
            @pl.when(sides[side][0])
            def _():
                arrived(term_in.at[array, side, col], term_recv.at[array, side, col])
        for row in range(rows):
            total = acc[array, row + 1, col]
            if row == 0:
                total = total + term_in[array, 0, col].astype(jnp.float32)
            if row == rows - 1:
                total = total + term_in[array, 1, col].astype(jnp.float32)
            kv_out[array, row, col] = total.astype(jnp.bfloat16)
            deliver(array + 1, row, col)

    def await_input(array, row, col):
        arrived(slot(array, row, col), in_recv.at[array, row * cols + col])

    def await_array(array):
        for row in range(rows):
            for col in range(cols):
                await_input(array, row, col)

    forward(0)
    spread(2)
    await_array(2)
    spread(3)
    await_halo(0, 0)
    for col in range(cols):
        await_halo(0, col + 1)
        for row in range(rows):
            softmax(row, col)
    forward(1)
    await_array(3)
    for col in range(cols):
        for row in range(rows):
            value_gradient(row, col)
        if col >= 1:
            send_terms(1, col - 1)
    send_terms(1, cols - 1)
    await_halo(1, 0)
    for col in range(cols):
        await_halo(1, col + 1)
        for row in range(rows):
            gradients(row, col)
        if col >= 1:
            send_terms(0, col - 1)
        if col == cols - 1:
            send_terms(0, col)
        finish(1, col)
        if col >= 2:
            finish(0, col - 2)
        for row in range(rows):
            deliver(0, row, col)
    for col in range(max(cols - 2, 0), cols):
        finish(0, col)

    for ref, array in inputs:
        for step in range(1, members):
            in_copy(ref, array, step).wait_send()
    for array in range(2):
        for side in range(2):
            for col in range(cols):
                @pl.when(sides[side][0])
                def _():
                    halo_copy(array, side, col).wait_send()
                    term_copy(array, side, col).wait_send()
    for array in range(3):
        for row in range(rows):
            for col in range(cols):
                @pl.when(me != row * cols + col)
                def _():
                    out_copy(array, row, col).wait_send()
        for member in range(members):
            arrived(chunk(outs[array], member), out_recv.at[array, member])


def flush_kernel(a_ref, b_ref, c_ref, a_out, b_out, c_out, sems):
    copies = [
        pltpu.make_async_copy(src, dst, sems.at[index])
        for index, (src, dst) in enumerate(((a_ref, a_out), (b_ref, b_out), (c_ref, c_out)))
    ]
    for copy in copies:
        copy.start()
    for copy in copies:
        copy.wait()


def shards(rows, cols, groups, queries, keys, values, grad_out):
    shape = queries.shape
    tokens, full = shape[2] * shape[3], shape[4]
    members = rows * cols
    width = full // members
    heads = width // HD

    def pack(array):
        array = array.reshape(tokens, full)
        if width % LANES == 0:
            return array
        return array.reshape(tokens, members, width).transpose(1, 0, 2)

    def unpack(array):
        if width % LANES:
            array = array.transpose(1, 0, 2)
        return array.reshape(shape)

    packed = (tokens, full) if width % LANES == 0 else (members, tokens, width)
    low, wide = jnp.bfloat16, jnp.float32
    dma = pltpu.SemaphoreType.DMA
    outputs = pl.pallas_call(
        functools.partial(attention_kernel, cols, rows, groups, tokens, width, heads),
        out_shape=[jax.ShapeDtypeStruct(packed, low)] * 3,
        in_specs=[pl.BlockSpec(memory_space=pl.ANY)] * 4,
        out_specs=[pl.BlockSpec(memory_space=pltpu.MemorySpace.VMEM)] * 3,
        scratch_shapes=[
            pltpu.VMEM((2, rows, cols, tokens, width), low),
            pltpu.VMEM((2, rows + 2, cols, tokens, width), low),
            pltpu.VMEM((2, rows + 2, cols, tokens, width), wide),
            pltpu.VMEM((rows, cols, 3, 3 * tokens, heads * tokens), wide),
            pltpu.VMEM((rows, cols, heads * tokens, width), low),
            pltpu.VMEM((rows, cols, heads * tokens, width), low),
            pltpu.VMEM((rows, cols, tokens, width), low),
            pltpu.VMEM((2, rows, cols, tokens, width), low),
            pltpu.VMEM((2, 2, cols, tokens, width), low),
            pltpu.VMEM((2, 2, cols, tokens, width), low),
            dma((4, members)),
            dma((4, members)),
            dma((2, 2, cols)),
            dma((2, 2, cols)),
            dma((2, 2, cols)),
            dma((2, 2, cols)),
            dma((3, rows, cols)),
            dma((3, members)),
        ],
        compiler_params=pltpu.CompilerParams(
            collective_id=0, has_side_effects=True, vmem_limit_bytes=62 * 1024 * 1024
        ),
    )(pack(queries), pack(keys), pack(values), pack(grad_out))
    outputs = pl.pallas_call(
        flush_kernel,
        out_shape=[jax.ShapeDtypeStruct(packed, low)] * 3,
        in_specs=[pl.BlockSpec(memory_space=pltpu.MemorySpace.VMEM)] * 3,
        out_specs=[pl.BlockSpec(memory_space=pl.ANY)] * 3,
        scratch_shapes=[dma((3,))],
        compiler_params=pltpu.CompilerParams(vmem_limit_bytes=62 * 1024 * 1024),
    )(*outputs)
    return tuple(unpack(array) for array in outputs)


def solution(mesh):
    cols, lines = mesh.shape["inline"], mesh.shape["xline"]
    spec = P("inline", "xline", None, None, None)

    def body(queries, keys, values, grad_out):
        heads = queries.shape[4] // HD
        rows = 2 if heads % (2 * cols) == 0 and lines % 2 == 0 else 1
        return shards(rows, cols, lines // rows, queries, keys, values, grad_out)

    return jax.shard_map(
        body, mesh=mesh, in_specs=(spec,) * 4, out_specs=(spec,) * 3, check_vma=False
    )
```
